256 devices in a mesh: front: 2 (over core), grid: 128 (over y, x, z).
Axes of the slice: x: 4, y: 4, z: 8, core: 2. Of those that a mesh axis runs over, the one named last changes fastest.
Arguments:
- child_schur: float32 [2, 2, 8192, 8192], P('front', None, 'grid'), as said below
- child_map: int32 [2, 2, 64], replicated, may hold values from 0 to 95, as said below
- orig_columns: float32 [2, 12288, 384], P('front', 'grid')
Outputs:
- factor_panel: float32 [2, 12288, 384], P('front', 'grid')
- schur_front: float32 [2, 12288, 12288], P('front', 'grid')
The draws below stay inside these ranges and needn't reach their ends.
Inputs may be any that keep to these rules, and one draw needn't show every extreme that they name: Each row child_map[p, k, :] is strictly increasing and holds 0 and 95. `child_schur`: each child front is symmetric; the first 384 rows of each orig_columns[p] form a symmetric block, and each first 384 rows of panel_block are symmetric positive definite.
All inputs are finite; a program needn't handle non-finite values.
Results may differ from the reference program's by a relative error of at most 0.0001.
Values sent between devices are 32-bit elements; how exact they have to be, the bound alone decides.
A program may use at most 128 MiB of HBM per device.

```python
import jax
import jax.numpy as jnp
from jax import lax

P_SIZE = 12288
C = 8192
NB = 384
BLK = 128
KIDS = 2
PARENTS = 2


def draw_child_schur(key, part):
    key = jax.random.fold_in(key, 11)
    entry_key, lift_key = jax.random.split(key)
    entries = jax.random.uniform(entry_key, (PARENTS, KIDS, C, C), jnp.float32, -1.0, 1.0)
    symmetric = 0.5 * (entries + jnp.swapaxes(entries, 2, 3))
    diagonal_lift = jax.random.uniform(lift_key, (PARENTS, KIDS, C), jnp.float32, 8.0, 24.0)
    identity = jnp.eye(C, dtype=jnp.float32)
    return symmetric + diagonal_lift[:, :, :, None] * identity


def draw_orig_columns(key, part):
    key = jax.random.fold_in(key, 12)
    entry_key, lift_key = jax.random.split(key)
    entries = jax.random.uniform(entry_key, (PARENTS, P_SIZE, NB), jnp.float32, -1.0, 1.0)
    pivot_rows = entries[:, :NB]
    diagonal_lift = jax.random.uniform(lift_key, (PARENTS, NB), jnp.float32, 40.0, 80.0)
    identity = jnp.eye(NB, dtype=jnp.float32)
    pivot_rows = 0.5 * (pivot_rows + jnp.swapaxes(pivot_rows, 1, 2)) + diagonal_lift[:, :, None] * identity
    return jnp.concatenate([pivot_rows, entries[:, NB:]], axis=1)


def draw_child_map(key, part):
    key = jax.random.fold_in(key, 13)
    blocks_parent = P_SIZE // BLK
    blocks_child = C // BLK

    def draw_row(row_key):
        shuffled = jax.random.permutation(row_key, blocks_parent - 2) + 1
        chosen = jnp.sort(shuffled[:blocks_child - 2]).astype(jnp.int32)
        return jnp.concatenate([jnp.zeros((1,), jnp.int32), chosen, jnp.full((1,), blocks_parent - 1, jnp.int32)])
    row_keys = jax.random.split(key, PARENTS * KIDS)
    return jax.vmap(draw_row)(row_keys).reshape(PARENTS, KIDS, blocks_child)


def setup_inputs(seed: int = 0) -> dict:
    streams_of = jax.random.split(jax.random.key(seed), 4)
    return {
        "child_schur": draw_child_schur(jax.random.fold_in(streams_of[3], 71), 0),
        "child_map": draw_child_map(jax.random.fold_in(streams_of[3], 71), 0),
        "orig_columns": draw_orig_columns(jax.random.fold_in(streams_of[3], 71), 0),
    }


def source_blocks(child_blocks):
    parent_ids = jnp.arange(P_SIZE // BLK, dtype=jnp.int32)
    matches = child_blocks[None, :] == parent_ids[:, None]
    present = jnp.any(matches, axis=1)
    child_ids = jnp.arange(child_blocks.shape[0], dtype=jnp.int32)
    anchor = jnp.sum(jnp.where(matches, child_ids[None, :], 0), axis=1).astype(jnp.int32)
    return (anchor, present)

def reference(child_schur, child_map, orig_columns):
    row_ids = jnp.arange(P_SIZE, dtype=jnp.int32)
    inner = row_ids >= NB
    factor_list = []
    schur_list = []
    for parent in range(PARENTS):
        assembled = jnp.zeros((P_SIZE, P_SIZE), jnp.float32)
        for child in range(KIDS):
            anchor, present = source_blocks(child_map[parent, child])
            child_front = child_schur[(parent + child) % PARENTS, child]
            picked = child_front.reshape(C // BLK, BLK, C)[anchor].reshape(P_SIZE, C)
            picked = picked.reshape(P_SIZE, C // BLK, BLK)[:, anchor].reshape(P_SIZE, P_SIZE)
            kept = jnp.repeat(present, BLK)
            assembled = assembled + jnp.where(kept[:, None] & kept[None, :], picked, jnp.float32(0.0))
        panel_block = assembled[:, :NB] + orig_columns[parent]
        pivot_factor = jnp.linalg.cholesky(panel_block[:NB])
        solved = jax.scipy.linalg.solve_triangular(pivot_factor, panel_block.T, lower=True).T
        pivot_rows = jnp.pad(pivot_factor, ((0, P_SIZE - NB), (0, 0)))
        factor = jnp.where((row_ids < NB)[:, None], pivot_rows, solved)
        product = jnp.dot(factor, factor.T, precision=lax.Precision.HIGHEST)
        schur_block = jnp.where(inner[:, None] & inner[None, :], assembled - product, jnp.float32(0.0))
        factor_list.append(factor)
        schur_list.append(schur_block)
    return (jnp.stack(factor_list), jnp.stack(schur_list))
```

```python
import functools

import jax
import jax.numpy as jnp
from jax import lax
from jax.experimental import pallas as pl
from jax.experimental.pallas import tpu as pltpu
from jax.sharding import PartitionSpec as P

NB = 384
BLK = 128
PROWS = 96
CROWS = 64
GRID_SHAPE = (4, 4, 8)
MESH = pl.DeviceIdType.MESH
HIGHEST = lax.Precision.HIGHEST


def scan_sources(map_ref, parent, anchor, present, blocks):
    for child in range(2):
        def step(block, at, child=child):
            found = (map_ref[parent, child, at] == block).astype(jnp.int32)
            anchor[child, block] = at
            present[child, block] = found
            return at + found
        lax.fori_loop(0, blocks, lambda b, at: jnp.minimum(step(b, at), map_ref.shape[2] - 1), jnp.int32(0))


def joined(even, odd, child):
    lanes = lax.broadcasted_iota(jnp.int32, even.shape, 1)
    if child == 0:
        return jnp.where(lanes < CROWS, even, pltpu.roll(odd, CROWS, 1))
    return jnp.where(lanes < CROWS, pltpu.roll(even, CROWS, 1), odd)


def comm_kernel(
    shape, map_ref, schur, orig, got, panels,
    anchor, present, first, second, tiles, spread, after_z, after_x, corner, orig_v, panel_v,
    swap_sem, load_sem, z_send, z_recv, z_own, x_send, x_recv, x_own, y_send, y_recv,
    p_send, p_recv, p_own,
):
    ny, nx, nz = shape
    count = ny * nx * nz
    front = lax.axis_index("front")
    grid = lax.axis_index("grid")
    y = grid // (nx * nz)
    x = lax.rem(grid // nz, nx)
    z = lax.rem(grid, nz)

    def at(yy, xx, zz):
        return (front, (yy * nx + xx) * nz + zz)

    barrier = pltpu.get_barrier_semaphore()
    other = (1 - front, grid)
    pl.semaphore_signal(barrier, inc=1, device_id=other, device_id_type=MESH)
    for by in range(1, nz):
        pl.semaphore_signal(barrier, inc=1, device_id=at(y, x, lax.rem(z + by, nz)), device_id_type=MESH)
    for by in range(1, nx):
        pl.semaphore_signal(barrier, inc=1, device_id=at(y, lax.rem(x + by, nx), z), device_id_type=MESH)
    for by in range(1, ny):
        pl.semaphore_signal(barrier, inc=1, device_id=at(lax.rem(y + by, ny), x, z), device_id_type=MESH)
    load = pltpu.make_async_copy(schur.at[0], first, load_sem.at[0])
    load.start()
    load_orig = pltpu.make_async_copy(orig, orig_v, load_sem.at[1])
    load_orig.start()
    pl.semaphore_wait(barrier, 1 + (nz - 1) + (nx - 1) + (ny - 1))
    swap = pltpu.make_async_remote_copy(
        src_ref=schur.at[1], dst_ref=second, send_sem=swap_sem.at[0], recv_sem=swap_sem.at[1],
        device_id=other, device_id_type=MESH,
    )
    swap.start()
    scan_sources(map_ref, front, anchor, present, count * PROWS // BLK)
    load.wait()
    swap.wait()
    for child, held in ((0, first), (1, second)):
        for i in range(tiles.shape[1]):
            tiles[child, i] = held[:, i * BLK:(i + 1) * BLK]

    chunks = list(range(ny // 2, 0, -1)) + list(range(ny // 2 + 1, ny)) + [0]
    offsets = sorted(range(1, nz), key=lambda by: -min(by, nz - by))
    groups = nx * nz // 4
    z_copies, x_copies, y_copies = {}, {}, []

    for c in chunks:
        yc = lax.rem(y + c, ny)

        def build(h, carry, yc=yc):
            for i in range(3):
                block = yc * (3 * groups) + 3 * h + i
                parts = []
                for child in range(2):
                    tile = tiles[child, anchor[child, block]]
                    parts.append(tile * present[child, block].astype(jnp.float32))
                turned = jnp.concatenate(parts, axis=0).T
                for q in range(4):
                    unit = 4 * i + q
                    device = 4 * h + unit // 3
                    spread[yc, device // nz, lax.rem(device, nz), unit % 3] = turned[32 * q:32 * q + 32]
            return carry

        lax.fori_loop(0, groups, build, 0)
        for n, by in enumerate(offsets):
            to = lax.rem(z + by, nz)
            copy = pltpu.make_async_remote_copy(
                src_ref=spread.at[yc, :, to], dst_ref=after_z.at[z, yc],
                send_sem=z_send.at[c, n], recv_sem=z_recv.at[c, n],
                device_id=at(y, x, to), device_id_type=MESH,
            )
            copy.start()
            z_copies[c, n] = copy
        own = pltpu.make_async_copy(spread.at[yc, :, z], after_z.at[z, yc], z_own.at[c])
        own.start()
        z_copies[c, "own"] = own

    def start_x(c):
        yc = lax.rem(y + c, ny)
        for n in range(len(offsets)):
            z_copies[c, n].wait_recv()
        z_copies[c, "own"].wait()
        land = got if c == 0 else after_x
        for by in range(1, nx):
            to = lax.rem(x + by, nx)
            copy = pltpu.make_async_remote_copy(
                src_ref=after_z.at[:, yc, to], dst_ref=land.at[yc, x],
                send_sem=x_send.at[c, by], recv_sem=x_recv.at[c, by],
                device_id=at(y, to, z), device_id_type=MESH,
            )
            copy.start()
            x_copies[c, by] = copy
        own = pltpu.make_async_copy(after_z.at[:, yc, x], land.at[yc, x], x_own.at[c])
        own.start()
        x_copies[c, "own"] = own

    def finish_x(c):
        for by in range(1, nx):
            x_copies[c, by].wait_recv()
        x_copies[c, "own"].wait()

    def start_y(c):
        finish_x(c)
        yc = lax.rem(y + c, ny)
        copy = pltpu.make_async_remote_copy(
            src_ref=after_x.at[yc], dst_ref=got.at[y],
            send_sem=y_send.at[c], recv_sem=y_recv.at[c],
            device_id=at(yc, x, z), device_id_type=MESH,
        )
        copy.start()
        y_copies.append(copy)

    for n, c in enumerate(chunks):
        start_x(c)
        if n > 0:
            start_y(chunks[n - 1])
    finish_x(0)
    for copy in y_copies:
        copy.wait_recv()

    loads = []
    for d in range(6):
        copy = pltpu.make_async_copy(
            got.at[d // (nx * nz), (d // nz) % nx, d % nz], corner.at[d], load_sem.at[2 + d]
        )
        copy.start()
        loads.append(copy)
    load_orig.wait()
    for copy in loads:
        copy.wait()
    for block in range(3):
        value = orig_v[:, BLK * block:BLK * (block + 1)]
        for child in range(2):
            a = anchor[child, block]
            pair = [corner[2 * a + i].reshape(PROWS, BLK) for i in range(2)]
            value = value + present[child, block].astype(jnp.float32) * joined(pair[0], pair[1], child)
        panel_v[block] = value

    own = pltpu.make_async_copy(panel_v, panels.at[:, y, x, z], p_own)
    own.start()

    axes = {"y": (ny, y), "x": (nx, x), "z": (nz, z)}

    def neighbour(axis, by):
        size, here = axes[axis]
        there = lax.rem(here + by + size, size)
        return at(*[there if axis == a else axes[a][1] for a in "yxz"])

    def steps(part, order):
        whole = []
        for axis in order:
            size, here = axes[axis]
            index = [slice(None) if a in whole else axes[a][1] for a in "yxz"]
            for s in range(size // 2):
                half = s == size // 2 - 1
                yield axis, s, half, index, len(whole)
            whole.append(axis)

    def block_ref(part, axis, index, i, half):
        full = [i if a == axis else index[n] for n, a in enumerate("yxz")]
        rows = slice(None) if half is None else pl.ds(half * (PROWS // 2), PROWS // 2)
        return panels.at[(part, *full, rows)]

    own.wait()
    orders = ("zxy", "xyz", "yzx")
    plans = [list(steps(part, order)) for part, order in enumerate(orders)]
    pending = [[], [], []]
    sent = []
    for turn in range(max(len(p) for p in plans)):
        for part in range(3):
            if turn >= len(plans[part]):
                continue
            axis, s, half, index, _ = plans[part][turn]
            for copy in pending[part]:
                copy.wait_recv()
            pending[part] = []
            size, here = axes[axis]
            for way, by in ((0, 1), (1, -1)):
                origin = lax.rem(here - by * s + size, size)
                block = block_ref(part, axis, index, origin, way if half else None)
                copy = pltpu.make_async_remote_copy(
                    src_ref=block, dst_ref=block,
                    send_sem=p_send.at[part, turn, way], recv_sem=p_recv.at[part, turn, way],
                    device_id=neighbour(axis, by), device_id_type=MESH,
                )
                copy.start()
                pending[part].append(copy)
                sent.append(copy)
    for part in range(3):
        for copy in pending[part]:
            copy.wait_recv()
    swap_done = list(z_copies.items())
    for key, copy in swap_done:
        if key[1] != "own":
            copy.wait_send()
    for key, copy in x_copies.items():
        if key[1] != "own":
            copy.wait_send()
    for copy in y_copies:
        copy.wait_send()
    for copy in sent:
        copy.wait_send()


def exchange(shape, child_map, schur, orig):
    ny, nx, nz = shape
    count = ny * nx * nz
    blocks = count * PROWS // BLK
    unit = (3, 32, BLK)
    turns = (ny + nx + nz) // 2
    dma = pltpu.SemaphoreType.DMA
    hbm = pl.BlockSpec(memory_space=pl.ANY)
    return pl.pallas_call(
        functools.partial(comm_kernel, shape),
        out_shape=(
            jax.ShapeDtypeStruct((ny, nx, nz) + unit, jnp.float32),
            jax.ShapeDtypeStruct((3, ny, nx, nz, PROWS, BLK), jnp.float32),
        ),
        in_specs=[pl.BlockSpec(memory_space=pltpu.SMEM), hbm, hbm],
        out_specs=(hbm, hbm),
        scratch_shapes=[
            pltpu.SMEM((2, blocks), jnp.int32),
            pltpu.SMEM((2, blocks), jnp.int32),
            pltpu.VMEM(schur.shape[1:], jnp.float32),
            pltpu.VMEM(schur.shape[1:], jnp.float32),
            pltpu.VMEM((2, schur.shape[2] // BLK, CROWS, BLK), jnp.float32),
            pltpu.VMEM((ny, nx, nz) + unit, jnp.float32),
            pltpu.VMEM((nz, ny, nx) + unit, jnp.float32),
            pltpu.VMEM((ny, nx, nz) + unit, jnp.float32),
            pltpu.VMEM((6,) + unit, jnp.float32),
            pltpu.VMEM((PROWS, NB), jnp.float32),
            pltpu.VMEM((3, PROWS, BLK), jnp.float32),
            dma((2,)), dma((8,)),
            dma((ny, nz)), dma((ny, nz)), dma((ny,)),
            dma((ny, nx)), dma((ny, nx)), dma((ny,)),
            dma((ny,)), dma((ny,)),
            dma((3, turns, 2)), dma((3, turns, 2)), dma,
        ],
        compiler_params=pltpu.CompilerParams(
            collective_id=0, has_side_effects=True, vmem_limit_bytes=48 * 1024 * 1024
        ),
    )(child_map, schur, orig)


def update_kernel(shape, map_ref, front_ref, got, panels, weight, out, anchor, present):
    ny, nx, nz = shape
    count = ny * nx * nz
    step = pl.program_id(0)
    wide = nz * PROWS

    @pl.when(step == 0)
    def _():
        scan_sources(map_ref, front_ref[0], anchor, present, count * PROWS // BLK)

    product = jnp.zeros((PROWS, wide), jnp.float32)
    for part in range(3):
        columns = panels[part, 0, 0].reshape(wide, BLK)
        product += lax.dot_general(
            weight[:, part * BLK:(part + 1) * BLK], columns, (((1,), (1,)), ((), ())),
            precision=HIGHEST, preferred_element_type=jnp.float32,
        )
    rows = front_ref[1] * PROWS + lax.broadcasted_iota(jnp.int32, (PROWS, BLK), 0)
    for i in range(wide // BLK):
        block = step * (wide // BLK) + i
        value = -product[:, i * BLK:(i + 1) * BLK]
        for child in range(2):
            a = anchor[child, block]
            pair = [got[2 * a + n].reshape(PROWS, BLK) for n in range(2)]
            value = value + present[child, block].astype(jnp.float32) * joined(pair[0], pair[1], child)
        inside = (rows >= NB) & (block >= NB // BLK)
        out[:, i * BLK:(i + 1) * BLK] = jnp.where(inside, value, 0.0)


def update(shape, child_map, where, got, panels, weight):
    ny, nx, nz = shape
    count = ny * nx * nz
    blocks = count * PROWS // BLK
    wide = nz * PROWS
    smem = pl.BlockSpec(memory_space=pltpu.SMEM)
    return pl.pallas_call(
        functools.partial(update_kernel, shape),
        grid=(ny * nx,),
        out_shape=jax.ShapeDtypeStruct((PROWS, count * PROWS), jnp.float32),
        in_specs=[
            smem, smem,
            pl.BlockSpec((count, 3, 32, BLK), lambda i: (0, 0, 0, 0)),
            pl.BlockSpec((3, 1, 1, nz, PROWS, BLK), lambda i: (0, i // nx, i % nx, 0, 0, 0)),
            pl.BlockSpec((PROWS, NB), lambda i: (0, 0)),
        ],
        out_specs=pl.BlockSpec((PROWS, wide), lambda i: (0, i)),
        scratch_shapes=[pltpu.SMEM((2, blocks), jnp.int32), pltpu.SMEM((2, blocks), jnp.int32)],
        compiler_params=pltpu.CompilerParams(vmem_limit_bytes=48 * 1024 * 1024),
    )(child_map, where, got.reshape(count, 3, 32, BLK), panels, weight)


def on_device(shape, child_schur, child_map, orig_columns):
    got, panels = exchange(shape, child_map, child_schur[0], orig_columns[0])
    count = shape[0] * shape[1] * shape[2]
    grid = lax.axis_index("grid")
    by_row = panels.reshape(3, count, PROWS, BLK)
    pivot_block = by_row[:, :NB // PROWS].reshape(3, NB, BLK).transpose(1, 0, 2).reshape(NB, NB)
    own_panel = lax.dynamic_index_in_dim(by_row, grid, 1, keepdims=False).transpose(1, 0, 2).reshape(PROWS, NB)
    pivot_factor = jnp.linalg.cholesky(pivot_block)
    inverse = jax.scipy.linalg.solve_triangular(pivot_factor, jnp.eye(NB, dtype=jnp.float32), lower=True)
    solved = jnp.dot(own_panel, inverse.T, precision=HIGHEST)
    row_ids = grid * PROWS + jnp.arange(PROWS, dtype=jnp.int32)
    pivot_rows = jnp.take(pivot_factor, jnp.clip(row_ids, 0, NB - 1), axis=0)
    factor = jnp.where((row_ids < NB)[:, None], pivot_rows, solved)
    weight = jnp.dot(solved, inverse, precision=HIGHEST)
    where = jnp.stack([lax.axis_index("front"), grid]).astype(jnp.int32)
    schur_block = update(shape, child_map, where, got, panels, weight)
    return (factor[None], schur_block[None])


def solution(mesh):
    placed = (P("front", None, "grid", None), P(), P("front", "grid", None))
    count = mesh.shape["grid"]
    shape = GRID_SHAPE if count == 128 else (count // 8, 2, 4)
    return jax.shard_map(
        functools.partial(on_device, shape),
        mesh=mesh,
        in_specs=placed,
        out_specs=(P("front", "grid", None), P("front", "grid", None)),
        check_vma=False,
    )
```
